256 devices in a mesh: fsdp: 32 (over x_lo, z, core), seq: 8 (over y, x_hi).
Axes of the slice: x: 4 (x_hi: 2, x_lo: 2; x = x_hi * 2 + x_lo), y: 4, z: 8, core: 2. Of those that a mesh axis runs over, the one named last changes fastest.
Arguments:
- queries: bfloat16 [32, 1024, 3072], P('fsdp', 'seq'), may hold values from -128 to 128
- keys: bfloat16 [32, 1024, 3072], P('fsdp', 'seq'), may hold values from -4 to 4
- values: bfloat16 [32, 1024, 3072], P('fsdp', 'seq'), may hold values from -5 to 5
- query_tangent: bfloat16 [32, 1024, 3072], P('fsdp', 'seq'), may hold values from -5 to 5
- key_tangent: bfloat16 [32, 1024, 3072], P('fsdp', 'seq'), may hold values from -5 to 5
- value_tangent: bfloat16 [32, 1024, 3072], P('fsdp', 'seq'), may hold values from -5 to 5
- out_weight: bfloat16 [3072, 6144], P('seq', 'fsdp'), may hold values from -0.109375 to 0.109375
Outputs:
- mixed: bfloat16 [32, 1024, 6144], P('fsdp', 'seq')
- mixed_tangent: bfloat16 [32, 1024, 6144], P('fsdp', 'seq')
The draws below stay inside these ranges and needn't reach their ends.
All inputs are finite; a program needn't handle non-finite values.
Results may differ from the reference program's by a relative error of at most 0.017.
Values may be sent and summed in bfloat16 or wider, within the bound.
A program may use at most 128 MiB of HBM per device.

```python
import math
import jax
import jax.numpy as jnp
from jax import lax

D = 6144
HEADS = 24
HD = 128
SEQLEN = 1024
CLIPS = 32
N_SEQ = 8


def pair_draw(key):
    key_query, key_key = jax.random.split(key, 2)
    shape = (CLIPS, SEQLEN, HEADS * HD)
    base_query = jax.random.truncated_normal(key_query, -4.0, 4.0, shape, jnp.float32)
    base_key = jax.random.truncated_normal(key_key, -4.0, 4.0, shape, jnp.float32)
    return (base_query, base_key)


def draw_queries(key, part):
    base_query, base_key = pair_draw(key)
    result = base_query
    return result.astype(jnp.bfloat16)


def draw_keys(key, part):
    base_query, base_key = pair_draw(key)
    result = base_key
    return result.astype(jnp.bfloat16)


def draw_key_tangent(key, part):
    key = jax.random.fold_in(key, 11)
    shape = (CLIPS, SEQLEN, HEADS * HD)
    result = jax.random.truncated_normal(key, -5.0, 5.0, shape, jnp.float32)
    return result.astype(jnp.bfloat16)


def level_of(rng, shape, cuts, smallest, top_value):
    factor_of, own = 1.0, jax.random.fold_in(rng, 6)
    for position, blocks in cuts:
        steps = jnp.exp(jax.random.uniform(jax.random.fold_in(own, position), (blocks,), jnp.float32, smallest / len(cuts), top_value / len(cuts)))
        factor_of = factor_of * jnp.repeat(steps, shape[position] // blocks).reshape([-1 if axis == position else 1 for axis in range(len(shape))])
    return factor_of


def scatter_about(own_key, shape, spread, bound, cuts=(), dtype=jnp.bfloat16):
    drawn = spread * jax.random.normal(own_key, shape, jnp.float32)
    if cuts:
        drawn = drawn * level_of(own_key, shape, cuts, -0.22, 0.18)
    return jnp.clip(drawn, -bound, bound).astype(dtype)


def setup_inputs(seed: int = 0) -> dict:
    streams_of = jax.random.split(jax.random.key(seed), 8)
    return {
        "queries": draw_queries(jax.random.fold_in(streams_of[7], 71), 0),
        "keys": draw_keys(jax.random.fold_in(streams_of[7], 71), 0),
        "values": scatter_about(streams_of[2], (CLIPS, SEQLEN, HEADS * HD), 1.0, 5.0, ((0, 32), (1, 8))),
        "query_tangent": scatter_about(streams_of[3], (CLIPS, SEQLEN, HEADS * HD), 1.0, 5.0, ((0, 32), (1, 8))),
        "key_tangent": draw_key_tangent(jax.random.fold_in(streams_of[7], 71), 0),
        "value_tangent": scatter_about(streams_of[5], (CLIPS, SEQLEN, HEADS * HD), 1.0, 5.0, ((0, 32), (1, 8))),
        "out_weight": scatter_about(streams_of[6], (HEADS * HD, D), (HEADS * HD) ** -0.5, 0.109375, ((0, 8), (1, 32))),
    }


def attend_head(pieces):
    query, key_rows, value_rows, query_dot, key_dot, value_dot = pieces
    scale = 1.0 / math.sqrt(query.shape[1])
    scores = jnp.dot(query, key_rows.T, preferred_element_type=jnp.float32) * scale
    scores_dot = (jnp.dot(query_dot, key_rows.T, preferred_element_type=jnp.float32) + jnp.dot(query, key_dot.T, preferred_element_type=jnp.float32)) * scale
    peak = lax.optimization_barrier(jnp.max(scores, axis=-1, keepdims=True))
    expo = jnp.exp(scores - peak)
    probs = expo / lax.optimization_barrier(jnp.sum(expo, axis=-1, keepdims=True))
    probs_dot = probs * (scores_dot - lax.optimization_barrier(jnp.sum(probs * scores_dot, axis=-1, keepdims=True)))
    probs_low = probs.astype(jnp.bfloat16)
    probs_dot_low = probs_dot.astype(jnp.bfloat16)
    out = jnp.dot(probs_low, value_rows, preferred_element_type=jnp.float32).astype(jnp.bfloat16)
    out_dot = (jnp.dot(probs_dot_low, value_rows, preferred_element_type=jnp.float32) + jnp.dot(probs_low, value_dot, preferred_element_type=jnp.float32)).astype(jnp.bfloat16)
    return (out, out_dot)

def clip_layer(pieces, out_weight):

    def split_heads(array):
        return array.reshape(SEQLEN, HEADS, HD).transpose(1, 0, 2)
    heads = tuple((split_heads(array) for array in pieces))
    out, out_dot = lax.map(attend_head, heads)
    out = out.transpose(1, 0, 2).reshape(SEQLEN, HEADS * HD)
    out_dot = out_dot.transpose(1, 0, 2).reshape(SEQLEN, HEADS * HD)
    width = HEADS // N_SEQ * HD
    total = jnp.zeros((SEQLEN, D), jnp.float32)
    total_dot = jnp.zeros((SEQLEN, D), jnp.float32)
    for group in range(N_SEQ):
        rows = out_weight[group * width:(group + 1) * width]
        term = jnp.dot(out[:, group * width:(group + 1) * width], rows, preferred_element_type=jnp.float32)
        term_dot = jnp.dot(out_dot[:, group * width:(group + 1) * width], rows, preferred_element_type=jnp.float32)
        term = lax.optimization_barrier(term.astype(jnp.bfloat16))
        term_dot = lax.optimization_barrier(term_dot.astype(jnp.bfloat16))
        total = total + term.astype(jnp.float32)
        total_dot = total_dot + term_dot.astype(jnp.float32)
    return (total.astype(jnp.bfloat16), total_dot.astype(jnp.bfloat16))

def reference(queries, keys, values, query_tangent, key_tangent, value_tangent, out_weight):

    def one_clip(pieces):
        return clip_layer(pieces, out_weight)
    mixed, mixed_tangent = lax.map(one_clip, (queries, keys, values, query_tangent, key_tangent, value_tangent))
    return (mixed, mixed_tangent)
```

```python
import math

import jax
import jax.numpy as jnp
from jax import lax
from jax.experimental import pallas as pl
from jax.experimental.pallas import tpu as pltpu
from jax.sharding import PartitionSpec as P

HD = 128
MESH = pl.DeviceIdType.MESH
F32 = jnp.float32
BF16 = jnp.bfloat16
SCALE = 1.0 / math.sqrt(HD)


def kernel(q, k, v, qd, kd, vd, w, mixed, mixed_dot, W, inb, stage, a_p, a_q, acc, ob, wx,
           in_send, in_recv, in_loc, out_send, out_recv, wsend, wrecv, osem):
    f, s = lax.axis_index("fsdp"), lax.axis_index("seq")
    xlo, z, c = f // 16, (f // 2) % 8, f % 2
    y, xhi = s // 2, s % 2
    x = xhi * 2 + xlo
    peer = 1 - c
    z4 = (z + 4) % 8

    def dev(dx=0, dy=0, dz=0, core=None):
        xx, yy, zz = (x + dx) % 4, (y + dy) % 4, (z + dz) % 8
        return ((xx % 2) * 16 + zz * 2 + (c if core is None else core), yy * 2 + xx // 2)

    mate = dev(core=peer)

    barrier = pltpu.get_barrier_semaphore()

    def greet(device):
        pl.semaphore_signal(barrier, inc=1, device_id=device, device_id_type=MESH)

    def greet_seq(j, carry):
        greet((f, (s + j) % 8))
        return carry

    def greet_z(j, carry):
        greet(dev(dz=j))
        return carry

    lax.fori_loop(1, 8, greet_seq, 0)
    lax.fori_loop(1, 8, greet_z, 0)
    greet(mate)
    greet(dev(dx=1))
    greet(dev(dx=3))
    pl.semaphore_wait(barrier, 17)

    count = [0]

    def push(part, device, sem=None):
        if sem is None:
            sem = count[0]
            count[0] += 1
        pltpu.make_async_remote_copy(
            src_ref=part, dst_ref=part, send_sem=wsend.at[sem], recv_sem=wrecv.at[sem],
            device_id=device, device_id_type=MESH,
        ).start()
        return sem

    sent = []

    def landed(part, sem):
        pltpu.make_async_copy(part, part, wrecv.at[sem]).wait()
        sent.append((part, sem))

    def landed_later(part, sem):
        sent.append((part, sem))

    arrays = (qd, q, k, kd, v, vd)

    def send_in(h):
        def to(j, carry):
            t = (s + j) % 8
            for i, ref in enumerate(arrays):
                pltpu.make_async_remote_copy(
                    src_ref=ref.at[0, :, pl.ds(pl.multiple_of(t * 384 + h * HD, HD), HD)],
                    dst_ref=inb.at[h, s, :, pl.ds(i * HD, HD)],
                    send_sem=in_send.at[h], recv_sem=in_recv.at[h],
                    device_id=(f, t), device_id_type=MESH,
                ).start()
            return carry

        lax.fori_loop(1, 8, to, 0)
        for i, ref in enumerate(arrays):
            pltpu.make_async_copy(
                ref.at[0, :, pl.ds(pl.multiple_of(s * 384 + h * HD, HD), HD)],
                inb.at[h, s, :, pl.ds(i * HD, HD)],
                in_loc.at[h],
            ).start()

    def wait_in(h):
        pltpu.make_async_copy(inb.at[h, pl.ds(0, 7)], inb.at[h, pl.ds(0, 7)], in_recv.at[h]).wait()
        pltpu.make_async_copy(inb.at[h, s], inb.at[h, s], in_loc.at[h]).wait()

    def attend(h):
        def block(b, carry):
            qq = inb[h, pl.ds(2 * b, 2), :, 0:256].reshape(256, 256)
            kk = inb[h, :, :, 256:512].reshape(1024, 256)
            vv = inb[h, :, :, 512:768].reshape(1024, 256)
            nt = (((1,), (1,)), ((), ()))
            scores = lax.dot_general(qq[:, 128:], kk[:, :128], nt, preferred_element_type=F32)
            scores_dot = lax.dot_general(qq, kk, nt, preferred_element_type=F32)
            peak = jnp.max(scores, axis=1, keepdims=True)
            expo = jnp.exp((scores - peak) * SCALE)
            inv = 1.0 / jnp.sum(expo, axis=1, keepdims=True)
            mean = jnp.sum(expo * scores_dot, axis=1, keepdims=True) * inv
            probs = expo * inv
            probs_dot = (expo * (inv * SCALE)) * (scores_dot - mean)
            both = jnp.dot(probs.astype(BF16), vv, preferred_element_type=F32)
            out_dot = both[:, 128:] + jnp.dot(probs_dot.astype(BF16), vv[:, :128], preferred_element_type=F32)
            stage[h, pl.ds(2 * b, 2), 0] = both[:, :128].astype(BF16).reshape(2, 128, HD)
            stage[h, pl.ds(2 * b, 2), 1] = out_dot.astype(BF16).reshape(2, 128, HD)
            return carry

        lax.fori_loop(0, 4, block, 0)

    def out_slot(h, t):
        if h == 2:
            return a_q.at[:, :, pl.ds(pl.multiple_of(t * HD, HD), HD)]
        return a_p.at[:, :, pl.ds(pl.multiple_of(t * 256 + h * HD, HD), HD)]

    def send_out(h):
        def to(j, carry):
            t = (s + j) % 8
            pltpu.make_async_remote_copy(
                src_ref=stage.at[h, t], dst_ref=out_slot(h, s),
                send_sem=out_send.at[h], recv_sem=out_recv.at[h],
                device_id=(f, t), device_id_type=MESH,
            ).start()
            return carry

        lax.fori_loop(1, 8, to, 0)
        out_slot(h, s)[...] = stage[h, s]

    def wait_out(h):
        pltpu.make_async_copy(stage.at[h, pl.ds(0, 7)], stage.at[h, pl.ds(0, 7)], out_recv.at[h]).wait()

    def lanes(xl):
        return pl.ds(pl.multiple_of(xl * 384, HD), 384)

    xm, xp = (x + 3) % 4, (x + 1) % 4
    ym, yp = (y + 3) % 4, (y + 1) % 4

    def prepare_send():
        for h in range(3):
            pltpu.make_async_remote_copy(
                src_ref=w.at[pl.ds(pl.multiple_of(h * 128 + peer * 64, 64), 64)], dst_ref=wx.at[h],
                send_sem=osem.at[1], recv_sem=osem.at[2],
                device_id=mate, device_id_type=MESH,
            ).start()

    def prepare():
        pltpu.make_async_copy(wx, wx, osem.at[2]).wait()
        row = lax.broadcasted_iota(jnp.int32, (192, 384), 0)
        lane = lax.broadcasted_iota(jnp.int32, (192, 384), 1)
        put_own = (lane == row + 192 * c).astype(BF16)
        put_other = (lane == row + 192 * peer).astype(BF16)
        for h in range(3):
            own = w[pl.ds(pl.multiple_of(h * 128 + c * 64, 64), 64), :]
            both = jnp.dot(own, put_own, preferred_element_type=F32)
            both += jnp.dot(wx[h], put_other, preferred_element_type=F32)
            W[z, y, xhi, h, c, :, lanes(xlo)] = both.astype(BF16)

    mine = lambda h: W.at[z, y, xhi, h, c, :, lanes(xlo)]

    q1 = []

    def q1_send():
        first = count[0]
        count[0] += 7

        def to(j, carry):
            push(mine(2), dev(dz=j), first + j - 1)
            return carry

        lax.fori_loop(1, 8, to, 0)
        q1.append(first)
        q1.append(push(mine(0), dev(dz=4)))
        q1.append(push(mine(1), dev(dz=4)))

    def q1_wait():
        def of(j, carry):
            part = W.at[(z + 8 - j) % 8, y, xhi, 2, c, :, lanes(xlo)]
            pltpu.make_async_copy(part, part, wrecv.at[q1[0] + j - 1]).wait()
            return carry

        lax.fori_loop(1, 8, of, 0)
        landed(W.at[z4, y, xhi, 0, c, :, lanes(xlo)], q1[1])
        landed(W.at[z4, y, xhi, 1, c, :, lanes(xlo)], q1[2])

    p1 = {}

    def p1_first():
        for j in (1, 3, 2):
            p1["a", j] = push(mine(0), dev(dx=j))
            p1["b", j] = push(mine(1), dev(dy=j))

    def p1_second():
        for j in (1, 3, 2):
            from_x, from_y = (x + 4 - j) % 4, (y + 4 - j) % 4
            landed(W.at[z, y, from_x // 2, 0, c, :, lanes(from_x % 2)], p1["a", j])
            landed(W.at[z, from_y, xhi, 1, c, :, lanes(xlo)], p1["b", j])
        for j in (1, 3, 2):
            p1["A", j] = push(W.at[z, y, :, 0, c], dev(dy=j))
            p1["B", j] = push(W.at[z, :, xhi, 1, c, :, lanes(xlo)], dev(dx=j))

    def p1_wait(kind):
        for j in (1, 3, 2):
            from_x, from_y = (x + 4 - j) % 4, (y + 4 - j) % 4
            if kind == "A":
                landed(W.at[z, from_y, :, 0, c], p1["A", j])
            else:
                landed(W.at[z, :, from_x // 2, 1, c, :, lanes(from_x % 2)], p1["B", j])

    ring = {}
    own_peer = {}

    def chunk(slab, h, half, core=None):
        return W.at[slab, pl.ds(2 * half, 2), :, h, c if core is None else core]

    def ring_start(h):
        for half in range(2):
            ring[0, 0, h, half] = push(chunk(z, h, half), dev(dz=1))
            ring[1, 0, h, half] = push(chunk(z, h, half), dev(dz=7))
        own_peer[h] = push(W.at[z, :, :, h, c], mate)

    def slab_of(way, step):
        return (z + 7 - step) % 8 if way == 0 else (z + 1 + step) % 8

    ring_peer = {}

    def ring_turn(step, h, half):
        for way in range(2):
            part = chunk(slab_of(way, step), h, half)
            landed(part, ring[way, step, h, half])
            if step < 2:
                ring[way, step + 1, h, half] = push(part, dev(dz=1 if way == 0 else 7))
            ring_peer[way, step, h, half] = push(part, mate)

    def ring_peer_wait(step):
        for way in range(2):
            for h in range(2):
                for half in range(2):
                    landed(chunk(slab_of(way, step), h, half, peer), ring_peer[way, step, h, half])

    q2 = {}
    group_slabs = {"a": 0, "b": 4}
    group_extra = {"a": 0, "b": 1}

    def parts(group, at, core, half=None):
        first, size, rows = group_slabs[group], 4, slice(None)
        if half is not None:
            first, size, rows = first + 2 * half, 2, pl.ds(32 * half, 32)
        yy, hh, ll = at
        return (W.at[pl.ds(first, size), yy, hh, 2, core, :, ll],
                W.at[z4, yy, hh, group_extra[group], core, rows, ll])

    whole = slice(None)

    def q2_push(key, group, at, device, half=None):
        q2[key] = [push(part, device) for part in parts(group, at, c, half)]

    def q2_landed(key, group, at, half=None, core=None):
        for part, sem in zip(parts(group, at, c if core is None else core, half), q2[key]):
            landed(part, sem)

    def at_x(xx):
        return (y, xx // 2, lanes(xx % 2))

    def at_y(yy):
        return (yy, xhi, lanes(xlo))

    def row_y(yy):
        return (yy, whole, whole)

    def column_x(xx):
        return (whole, xx // 2, lanes(xx % 2))

    plan = {"a": (at_x, x, xm, xp, "x", row_y, y, ym, yp, "y"),
            "b": (at_y, y, ym, yp, "y", column_x, x, xm, xp, "x")}

    def step_to(axis, up):
        return dev(dx=1 if up else 3) if axis == "x" else dev(dy=1 if up else 3)

    def q2_1():
        for g in "ab":
            one, me, lo, hi, axis = plan[g][:5]
            q2_push((g, 1, "up"), g, one(me), step_to(axis, True))
            q2_push((g, 1, "down"), g, one(me), step_to(axis, False))

    def q2_2():
        for g in "ab":
            one, me, lo, hi, axis = plan[g][:5]
            q2_landed((g, 1, "up"), g, one(lo))
            q2_push((g, 2, "up"), g, one(lo), step_to(axis, True), 0)
            q2_landed((g, 1, "down"), g, one(hi))
            q2_push((g, 2, "down"), g, one(hi), step_to(axis, False), 1)

    def q2_3():
        for g in "ab":
            one, me, lo, hi, axis, many, me2, lo2, hi2, axis2 = plan[g]
            q2_landed((g, 2, "up"), g, one((me + 2) % 4), 0)
            q2_landed((g, 2, "down"), g, one((me + 2) % 4), 1)
            q2_push((g, 3, "up"), g, many(me2), step_to(axis2, True))
            q2_push((g, 3, "down"), g, many(me2), step_to(axis2, False))
            q2_push((g, "peer", 0), g, many(me2), mate)

    def q2_4():
        for g in "ab":
            many, me2, lo2, hi2, axis2 = plan[g][5:]
            q2_landed((g, 3, "up"), g, many(lo2))
            q2_push((g, 4, "up"), g, many(lo2), step_to(axis2, True), 0)
            q2_landed((g, 3, "down"), g, many(hi2))
            q2_push((g, 4, "down"), g, many(hi2), step_to(axis2, False), 1)
            q2_push((g, "peer", 3), g, many(lo2), mate)
            q2_push((g, "peer", 1), g, many(hi2), mate)

    def q2_5():
        for g in "ab":
            many, me2 = plan[g][5:7]
            q2_landed((g, 4, "up"), g, many((me2 + 2) % 4), 0)
            q2_landed((g, 4, "down"), g, many((me2 + 2) % 4), 1)
            q2_push((g, "peer", 2), g, many((me2 + 2) % 4), mate)

    def q2_peer_wait():
        for g in "ab":
            many, me2 = plan[g][5:7]
            for j in range(4):
                q2_landed((g, "peer", j), g, many((me2 + j) % 4), core=peer)

    def project(n):
        wide = W[n, :, :, 0:2].reshape(2048, 768)
        acc[n] = jnp.dot(a_p[...].reshape(256, 2048), wide, preferred_element_type=F32)

    def finish(n, carry):
        wide = W[n, :, :, 2].reshape(1024, 768)
        total = acc[n] + jnp.dot(a_q[...].reshape(256, 1024), wide, preferred_element_type=F32)
        ob[n] = total.astype(BF16).reshape(2, 128, 768)
        for i, ref in enumerate((mixed, mixed_dot)):
            for xl in range(2):
                pltpu.make_async_copy(
                    ob.at[n, i, :, pl.ds(xl * 384, 384)],
                    ref.at[0, :, pl.ds(pl.multiple_of(xl * 3072 + n * 384, HD), 384)],
                    osem.at[0],
                ).start()
        return carry

    def project_pair(step):
        def one(way, carry):
            project((z + 7 - step + way * (2 + 2 * step)) % 8)
            return carry

        lax.fori_loop(0, 2, one, 0)

    prepare_send()
    prepare()
    p1_first()
    q1_send()
    send_in(0)
    p1_second()
    send_in(1)
    p1_wait("A")
    ring_start(0)
    p1_wait("B")
    ring_start(1)
    send_in(2)
    wait_in(0)
    attend(0)
    send_out(0)
    q1_wait()
    wait_in(1)
    q2_1()
    attend(1)
    send_out(1)
    for h in range(2):
        for half in range(2):
            ring_turn(0, h, half)
    q2_2()
    wait_in(2)
    attend(2)
    send_out(2)
    q2_3()
    wait_out(0)
    wait_out(1)
    for h in range(2):
        landed(W.at[z, :, :, h, peer], own_peer[h])
    project(z)
    ring_peer_wait(0)
    for h in range(2):
        for half in range(2):
            ring_turn(1, h, half)
    project_pair(0)
    q2_4()
    ring_peer_wait(1)
    project_pair(1)
    wait_out(2)
    q2_5()
    for h in range(2):
        for half in range(2):
            ring_turn(2, h, half)
    q2_peer_wait()
    project(z4)
    ring_peer_wait(2)
    project_pair(2)
    lax.fori_loop(0, 8, finish, 0)

    pltpu.make_async_copy(ob, ob, osem.at[0]).wait()
    pltpu.make_async_copy(wx, wx, osem.at[1]).wait()
    for h in range(3):
        pltpu.make_async_copy(inb.at[h, pl.ds(0, 7)], inb.at[h, pl.ds(0, 7)], in_send.at[h]).wait()
        pltpu.make_async_copy(stage.at[h, pl.ds(0, 7)], stage.at[h, pl.ds(0, 7)], out_send.at[h]).wait()

    def left(j, carry):
        pltpu.make_async_copy(mine(2), mine(2), wsend.at[q1[0] + j]).wait()
        return carry

    lax.fori_loop(0, 7, left, 0)
    for part, sem in sent:
        pltpu.make_async_copy(part, part, wsend.at[sem]).wait()
    assert count[0] <= wsend.shape[0] and len(sent) == count[0] - 7


def body(queries, keys, values, query_tangent, key_tangent, value_tangent, out_weight):
    any_space = pl.BlockSpec(memory_space=pl.ANY)
    shape = jax.ShapeDtypeStruct((1, 128, 6144), BF16)
    return pl.pallas_call(
        kernel,
        name="attend_project",
        out_shape=(shape, shape),
        in_specs=[any_space] * 6 + [pl.BlockSpec(memory_space=pltpu.VMEM)],
        out_specs=(any_space, any_space),
        scratch_shapes=[
            pltpu.VMEM((8, 4, 2, 3, 2, 64, 768), BF16),
            pltpu.VMEM((3, 8, 128, 768), BF16),
            pltpu.VMEM((3, 8, 2, 128, 128), BF16),
            pltpu.VMEM((2, 128, 2048), BF16),
            pltpu.VMEM((2, 128, 1024), BF16),
            pltpu.VMEM((8, 256, 768), F32),
            pltpu.VMEM((8, 2, 128, 768), BF16),
            pltpu.VMEM((3, 64, 192), BF16),
            pltpu.SemaphoreType.DMA((3,)),
            pltpu.SemaphoreType.DMA((3,)),
            pltpu.SemaphoreType.DMA((3,)),
            pltpu.SemaphoreType.DMA((3,)),
            pltpu.SemaphoreType.DMA((3,)),
            pltpu.SemaphoreType.DMA((160,)),
            pltpu.SemaphoreType.DMA((160,)),
            pltpu.SemaphoreType.DMA((3,)),
        ],
        compiler_params=pltpu.CompilerParams(
            collective_id=0, has_side_effects=True, vmem_limit_bytes=62 * 2**20
        ),
        cost_estimate=pl.CostEstimate(
            flops=17 * 10**9, bytes_accessed=8 * 2**20, transcendentals=3 * 2**20
        ),
    )(queries, keys, values, query_tangent, key_tangent, value_tangent, out_weight)


def solution(mesh):
    placed = (P("fsdp", "seq", None),) * 6 + (P("seq", "fsdp"),)
    return jax.shard_map(
        body,
        mesh=mesh,
        in_specs=placed,
        out_specs=(P("fsdp", "seq", None), P("fsdp", "seq", None)),
        check_vma=False,
    )
```

```python
import math

import jax
import jax.numpy as jnp
from jax import lax
from jax.experimental import pallas as pl
from jax.experimental.pallas import tpu as pltpu
from jax.sharding import PartitionSpec as P

HD = 128
MESH = pl.DeviceIdType.MESH
F32 = jnp.float32
BF16 = jnp.bfloat16
SCALE = 1.0 / math.sqrt(HD)
TURNS = (0, 1, 3, 2)


def kernel(q, k, v, qd, kd, vd, w, mixed, mixed_dot, W, inb, stage, A, ob, wx,
           in_send, in_recv, in_loc, out_send, out_recv, fsend, frecv, wsend, wrecv, osem):
    f, s = lax.axis_index("fsdp"), lax.axis_index("seq")
    xlo, z, c = f // 16, (f // 2) % 8, f % 2
    y, xhi = s // 2, s % 2
    x = xhi * 2 + xlo
    peer = 1 - c
    xm, xp = (x + 3) % 4, (x + 1) % 4

    def dev(dx=0, dy=0, dz=0, core=None):
        xx, yy, zz = (x + dx) % 4, (y + dy) % 4, (z + dz) % 8
        return ((xx % 2) * 16 + zz * 2 + (c if core is None else core), yy * 2 + xx // 2)

    mate = dev(core=peer)

    barrier = pltpu.get_barrier_semaphore()

    def greet(device):
        pl.semaphore_signal(barrier, inc=1, device_id=device, device_id_type=MESH)

    def greet_seq(j, carry):
        greet((f, (s + j) % 8))
        return carry

    def greet_x(j, carry):
        greet(dev(dx=1, dy=j))
        greet(dev(dx=3, dy=j))
        return carry

    lax.fori_loop(1, 8, greet_seq, 0)
    lax.fori_loop(0, 4, greet_x, 0)
    greet(dev(dz=1))
    greet(dev(dz=7))
    greet(mate)
    pl.semaphore_wait(barrier, 18)

    count = [0]
    sent = []

    def push(part, device):
        sem = count[0]
        count[0] += 1
        pltpu.make_async_remote_copy(
            src_ref=part, dst_ref=part, send_sem=wsend.at[sem], recv_sem=wrecv.at[sem],
            device_id=device, device_id_type=MESH,
        ).start()
        return sem

    def landed(part, sem):
        pltpu.make_async_copy(part, part, wrecv.at[sem]).wait()
        sent.append((part, sem))

    arrays = (qd, q, k, kd, v, vd)

    def send_in(h):
        def to(j, carry):
            t = (s + j) % 8
            for i, ref in enumerate(arrays):
                pltpu.make_async_remote_copy(
                    src_ref=ref.at[0, :, pl.ds(pl.multiple_of(t * 384 + h * HD, HD), HD)],
                    dst_ref=inb.at[h, s, :, pl.ds(i * HD, HD)],
                    send_sem=in_send.at[h], recv_sem=in_recv.at[h],
                    device_id=(f, t), device_id_type=MESH,
                ).start()
            return carry

        lax.fori_loop(1, 8, to, 0)
        for i, ref in enumerate(arrays):
            pltpu.make_async_copy(
                ref.at[0, :, pl.ds(pl.multiple_of(s * 384 + h * HD, HD), HD)],
                inb.at[h, s, :, pl.ds(i * HD, HD)],
                in_loc.at[h],
            ).start()

    def wait_in(h):
        pltpu.make_async_copy(inb.at[h, pl.ds(0, 7)], inb.at[h, pl.ds(0, 7)], in_recv.at[h]).wait()
        pltpu.make_async_copy(inb.at[h, s], inb.at[h, s], in_loc.at[h]).wait()

    def lane_of(h, hi, yy):
        return pl.ds(pl.multiple_of(((h * 2 + hi) * 4 + yy) * HD, HD), HD)

    def lanes_of(h, hi):
        return pl.ds(pl.multiple_of((h * 2 + hi) * 512, 512), 512)

    def send_out(h, yy):
        mine = lane_of(h, xhi, y)

        @pl.when(yy == y)
        def _():
            A[0:2, :, mine] = stage[h, yy, xhi]

        @pl.when(yy != y)
        def _():
            pltpu.make_async_remote_copy(
                src_ref=stage.at[h, yy, xhi], dst_ref=A.at[pl.ds(0, 2), :, mine],
                send_sem=out_send.at[h, 0], recv_sem=out_recv.at[h, 0],
                device_id=(f, yy * 2 + xhi), device_id_type=MESH,
            ).start()

        for row, sem, xx in ((0, 1, xm), (1, 2, xp)):
            pltpu.make_async_remote_copy(
                src_ref=stage.at[h, yy, 1 - xhi, row], dst_ref=A.at[row + 2, :, mine],
                send_sem=out_send.at[h, sem], recv_sem=out_recv.at[h, sem],
                device_id=((xx % 2) * 16 + z * 2 + c, yy * 2 + xx // 2), device_id_type=MESH,
            ).start()

    def attend(h):
        def block(b, carry):
            yy = (y + 1 + b) % 4
            qq = inb[h, pl.ds(2 * yy, 2), :, 0:256].reshape(256, 256)
            kk = inb[h, :, :, 256:512].reshape(1024, 256)
            vv = inb[h, :, :, 512:768].reshape(1024, 256)
            nt = (((1,), (1,)), ((), ()))
            scores = lax.dot_general(qq[:, 128:], kk[:, :128], nt, preferred_element_type=F32)
            scores_dot = lax.dot_general(qq, kk, nt, preferred_element_type=F32)
            peak = jnp.max(scores, axis=1, keepdims=True)
            expo = jnp.exp((scores - peak) * SCALE)
            inv = 1.0 / jnp.sum(expo, axis=1, keepdims=True)
            mean = jnp.sum(expo * scores_dot, axis=1, keepdims=True) * inv
            probs = expo * inv
            probs_dot = (expo * (inv * SCALE)) * (scores_dot - mean)
            both = jnp.dot(probs.astype(BF16), vv, preferred_element_type=F32)
            out_dot = both[:, 128:] + jnp.dot(probs_dot.astype(BF16), vv[:, :128], preferred_element_type=F32)
            stage[h, yy, :, 0] = both[:, :128].astype(BF16).reshape(2, 128, HD)
            stage[h, yy, :, 1] = out_dot.astype(BF16).reshape(2, 128, HD)
            send_out(h, yy)
            return carry

        lax.fori_loop(0, 4, block, 0)

    def wait_bytes(part, sem):
        pltpu.make_async_copy(part, part, sem).wait()

    def forward(h, i, src_row, dst_row, hi, dx):
        pltpu.make_async_remote_copy(
            src_ref=A.at[src_row, :, lanes_of(h, hi)], dst_ref=A.at[dst_row, :, lanes_of(h, hi)],
            send_sem=fsend.at[h, i], recv_sem=frecv.at[h, i],
            device_id=dev(dx=dx), device_id_type=MESH,
        ).start()

    def relay_out(h):
        wait_bytes(stage.at[h, pl.ds(0, 3), 0], out_recv.at[h, 0])
        forward(h, 0, 0, 2, xhi, 1)
        forward(h, 1, 1, 3, xhi, 3)
        wait_bytes(A.at[2, :, lanes_of(h, xp // 2)], out_recv.at[h, 1])
        forward(h, 2, 2, 0, xp // 2, 3)
        wait_bytes(A.at[3, :, lanes_of(h, xm // 2)], out_recv.at[h, 2])
        forward(h, 3, 3, 1, xm // 2, 1)

    def wait_out(h):
        wait_bytes(A.at[2, :, lanes_of(h, xm // 2)], frecv.at[h, 0])
        wait_bytes(A.at[3, :, lanes_of(h, xp // 2)], frecv.at[h, 1])
        wait_bytes(A.at[0, :, lanes_of(h, 1 - xhi)], frecv.at[h, 2])
        wait_bytes(A.at[1, :, lanes_of(h, 1 - xhi)], frecv.at[h, 3])

    def prepare_send():
        pltpu.make_async_remote_copy(
            src_ref=w.at[:, peer], dst_ref=wx, send_sem=osem.at[1], recv_sem=osem.at[2],
            device_id=mate, device_id_type=MESH,
        ).start()

    def prepare():
        wait_bytes(wx, osem.at[2])
        row = lax.broadcasted_iota(jnp.int32, (192, 384), 0)
        lane = lax.broadcasted_iota(jnp.int32, (192, 384), 1)
        put_own = (lane == row + 192 * c).astype(BF16)
        put_other = (lane == row + 192 * peer).astype(BF16)
        own = w[:, c].reshape(192, 192)
        both = jnp.dot(own, put_own, preferred_element_type=F32)
        both += jnp.dot(wx[...].reshape(192, 192), put_other, preferred_element_type=F32)
        W[z, :, xhi, y, c] = both.astype(BF16).reshape(3, 64, 384)

    def chunk(slab, turn, core=None):
        return W.at[slab, :, :, (y + turn) % 4, c if core is None else core]

    plane = {}
    ring = {}
    mates = {}

    def plane_x():
        plane["x"] = push(W.at[z, :, xhi, y, c], dev(dx=2))

    def plane_y():
        landed(W.at[z, :, 1 - xhi, y, c], plane["x"])
        for turn in (1, 3, 2):
            plane[turn] = push(chunk(z, 0), dev(dy=4 - turn))

    def ring_start(j):
        turn = TURNS[j]
        if turn:
            landed(chunk(z, turn), plane[turn])
        ring[0, 0, j] = push(chunk(z, turn), dev(dz=1))
        ring[1, 0, j] = push(chunk(z, turn), dev(dz=7))
        mates["own", j] = push(chunk(z, turn), mate)

    def slab_of(way, step):
        return (z + 7 - step) % 8 if way == 0 else (z + 1 + step) % 8

    def ways(step, j):
        return (0, 1) if step < 3 else ((0,) if j < 2 else (1,))

    def ring_turn(step, j):
        for way in ways(step, j):
            part = chunk(slab_of(way, step), TURNS[j])
            landed(part, ring[way, step, j])
            if step < 3 and way in ways(step + 1, j):
                ring[way, step + 1, j] = push(part, dev(dz=1 if way == 0 else 7))
            mates[way, step, j] = push(part, mate)

    def slab_wait(way, step):
        for j in range(4):
            if step is None:
                landed(chunk(z, TURNS[j], peer), mates["own", j])
            elif step < 3:
                landed(chunk(slab_of(way, step), TURNS[j], peer), mates[way, step, j])
            else:
                own_way = ways(3, j)[0]
                landed(chunk(slab_of(own_way, 3), TURNS[j], peer), mates[own_way, 3, j])

    def project(n):
        total = jnp.dot(A[...].reshape(512, 3072), W[n].reshape(3072, 384), preferred_element_type=F32)
        ob[n] = total.astype(BF16).reshape(4, 128, 384)
        columns = pl.ds(pl.multiple_of(xlo * 3072 + n * 384, HD), 384)
        for row, ref, dx in ((2, mixed, 3), (3, mixed_dot, 1)):
            pltpu.make_async_remote_copy(
                src_ref=ob.at[n, row], dst_ref=ref.at[0, :, columns],
                send_sem=osem.at[3], recv_sem=osem.at[4],
                device_id=dev(dx=dx), device_id_type=MESH,
            ).start()
        for row, ref in ((0, mixed), (1, mixed_dot)):
            pltpu.make_async_copy(ob.at[n, row], ref.at[0, :, columns], osem.at[0]).start()

    def project_pair(step):
        def one(way, carry):
            project((z + 7 - step + way * (2 + 2 * step)) % 8)
            return carry

        lax.fori_loop(0, 2, one, 0)

    prepare_send()
    prepare()
    plane_x()
    plane_y()
    ring_start(0)
    send_in(0)
    send_in(1)
    send_in(2)
    ring_start(1)
    ring_start(2)
    ring_start(3)
    ring_turn(0, 0)
    ring_turn(0, 1)
    wait_in(0)
    attend(0)
    ring_turn(0, 2)
    ring_turn(0, 3)
    ring_turn(1, 0)
    relay_out(0)
    ring_turn(1, 1)
    wait_in(1)
    attend(1)
    ring_turn(1, 2)
    ring_turn(1, 3)
    relay_out(1)
    wait_in(2)
    attend(2)
    ring_turn(2, 0)
    ring_turn(2, 1)
    relay_out(2)
    slab_wait(0, None)
    for h in range(3):
        wait_out(h)
    project(z)
    ring_turn(2, 2)
    slab_wait(0, 0)
    slab_wait(1, 0)
    project_pair(0)
    ring_turn(2, 3)
    slab_wait(0, 1)
    slab_wait(1, 1)
    project_pair(1)
    slab_wait(0, 2)
    slab_wait(1, 2)
    project_pair(2)
    for j in range(4):
        ring_turn(3, j)
    slab_wait(0, 3)
    project((z + 4) % 8)

    wait_bytes(ob.at[:, pl.ds(0, 2)], osem.at[4])
    wait_bytes(ob.at[:, pl.ds(0, 2)], osem.at[3])
    wait_bytes(ob.at[:, pl.ds(0, 2)], osem.at[0])
    wait_bytes(wx, osem.at[1])
    for h in range(3):
        wait_bytes(inb.at[h, pl.ds(0, 7)], in_send.at[h])
        wait_bytes(stage.at[h, pl.ds(0, 3), 0], out_send.at[h, 0])
        for i in (1, 2):
            wait_bytes(A.at[2, :, lanes_of(h, 0)], out_send.at[h, i])
        for i in range(4):
            wait_bytes(A.at[0, :, lanes_of(h, 0)], fsend.at[h, i])
    for part, sem in sent:
        wait_bytes(part, wsend.at[sem])
    assert count[0] <= wsend.shape[0] and len(sent) == count[0]


def body(queries, keys, values, query_tangent, key_tangent, value_tangent, out_weight):
    any_space = pl.BlockSpec(memory_space=pl.ANY)
    shape = jax.ShapeDtypeStruct((1, 128, 6144), BF16)
    return pl.pallas_call(
        kernel,
        name="attend_project",
        out_shape=(shape, shape),
        in_specs=[any_space] * 6 + [pl.BlockSpec(memory_space=pltpu.VMEM)],
        out_specs=(any_space, any_space),
        scratch_shapes=[
            pltpu.VMEM((8, 3, 2, 4, 2, 64, 384), BF16),
            pltpu.VMEM((3, 8, 128, 768), BF16),
            pltpu.VMEM((3, 4, 2, 2, 128, 128), BF16),
            pltpu.VMEM((4, 128, 3072), BF16),
            pltpu.VMEM((8, 4, 128, 384), BF16),
            pltpu.VMEM((3, 64, 192), BF16),
            pltpu.SemaphoreType.DMA((3,)),
            pltpu.SemaphoreType.DMA((3,)),
            pltpu.SemaphoreType.DMA((3,)),
            pltpu.SemaphoreType.DMA((3, 3)),
            pltpu.SemaphoreType.DMA((3, 3)),
            pltpu.SemaphoreType.DMA((3, 4)),
            pltpu.SemaphoreType.DMA((3, 4)),
            pltpu.SemaphoreType.DMA((96,)),
            pltpu.SemaphoreType.DMA((96,)),
            pltpu.SemaphoreType.DMA((5,)),
        ],
        compiler_params=pltpu.CompilerParams(
            collective_id=0, has_side_effects=True, vmem_limit_bytes=56 * 2**20
        ),
        cost_estimate=pl.CostEstimate(
            flops=17 * 10**9, bytes_accessed=8 * 2**20, transcendentals=3 * 2**20
        ),
    )(queries, keys, values, query_tangent, key_tangent, value_tangent, out_weight.reshape(3, 2, 64, 192))


def solution(mesh):
    placed = (P("fsdp", "seq", None),) * 6 + (P("seq", "fsdp"),)
    return jax.shard_map(
        body,
        mesh=mesh,
        in_specs=placed,
        out_specs=(P("fsdp", "seq", None), P("fsdp", "seq", None)),
        check_vma=False,
    )
```

```python
import math

import jax
import jax.numpy as jnp
from jax import lax
from jax.experimental import pallas as pl
from jax.experimental.pallas import tpu as pltpu
from jax.sharding import PartitionSpec as P

HD = 128
MESH = pl.DeviceIdType.MESH
F32 = jnp.float32
BF16 = jnp.bfloat16
SCALE = 1.0 / math.sqrt(HD)
TURNS = (0, 1, 3, 2)


def kernel(q, k, v, qd, kd, vd, w, mixed, mixed_dot, W, inb, stage, A, ob, wx, wo, wide,
           in_send, in_recv, in_loc, out_send, out_recv, fsend, frecv, wsend, wrecv, osem):
    f, s = lax.axis_index("fsdp"), lax.axis_index("seq")
    xlo, z, c = f // 16, (f // 2) % 8, f % 2
    y, xhi = s // 2, s % 2
    x = xhi * 2 + xlo
    peer = 1 - c
    xm, xp = (x + 3) % 4, (x + 1) % 4

    def dev(dx=0, dy=0, dz=0, core=None):
        xx, yy, zz = (x + dx) % 4, (y + dy) % 4, (z + dz) % 8
        return ((xx % 2) * 16 + zz * 2 + (c if core is None else core), yy * 2 + xx // 2)

    mate = dev(core=peer)

    barrier = pltpu.get_barrier_semaphore()

    def greet(device):
        pl.semaphore_signal(barrier, inc=1, device_id=device, device_id_type=MESH)

    def greet_seq(j, carry):
        greet((f, (s + j) % 8))
        return carry

    def greet_x(j, carry):
        greet(dev(dx=1, dy=j))
        greet(dev(dx=3, dy=j))
        return carry

    lax.fori_loop(1, 8, greet_seq, 0)
    lax.fori_loop(0, 4, greet_x, 0)
    greet(dev(dz=1))
    greet(dev(dz=7))
    greet(mate)
    pl.semaphore_wait(barrier, 18)

    count = [0]
    sent = []

    def push(part, device):
        sem = count[0]
        count[0] += 1
        pltpu.make_async_remote_copy(
            src_ref=part, dst_ref=part, send_sem=wsend.at[sem], recv_sem=wrecv.at[sem],
            device_id=device, device_id_type=MESH,
        ).start()
        return sem

    def landed(part, sem):
        pltpu.make_async_copy(part, part, wrecv.at[sem]).wait()
        sent.append((part, sem))

    arrays = (qd, q, k, kd, v, vd)

    def send_in_to(h, t):
        for i, ref in enumerate(arrays):
            pltpu.make_async_remote_copy(
                src_ref=ref.at[0, :, pl.ds(pl.multiple_of(t * 384 + h * HD, HD), HD)],
                dst_ref=inb.at[h, s, :, pl.ds(i * HD, HD)],
                send_sem=in_send.at[h], recv_sem=in_recv.at[h],
                device_id=(f, t), device_id_type=MESH,
            ).start()

    def send_in_x(h):
        send_in_to(h, 2 * y + 1 - xhi)

    def send_in(h):
        def to(j, carry):
            send_in_to(h, (2 * y + j) % 8)
            return carry

        lax.fori_loop(2, 8, to, 0)
        for i, ref in enumerate(arrays):
            pltpu.make_async_copy(
                ref.at[0, :, pl.ds(pl.multiple_of(s * 384 + h * HD, HD), HD)],
                inb.at[h, s, :, pl.ds(i * HD, HD)],
                in_loc.at[h],
            ).start()

    def wait_in(h):
        pltpu.make_async_copy(inb.at[h, pl.ds(0, 7)], inb.at[h, pl.ds(0, 7)], in_recv.at[h]).wait()
        pltpu.make_async_copy(inb.at[h, s], inb.at[h, s], in_loc.at[h]).wait()

    def lane_of(h, hi, yy):
        return pl.ds(pl.multiple_of(((h * 2 + hi) * 4 + yy) * HD, HD), HD)

    def lanes_of(h, hi):
        return pl.ds(pl.multiple_of((h * 2 + hi) * 512, 512), 512)

    def send_out(h, yy):
        mine = lane_of(h, xhi, y)

        @pl.when(yy == y)
        def _():
            A[0:2, :, mine] = stage[h, yy, xhi]

        @pl.when(yy != y)
        def _():
            pltpu.make_async_remote_copy(
                src_ref=stage.at[h, yy, xhi], dst_ref=A.at[pl.ds(0, 2), :, mine],
                send_sem=out_send.at[h, 0], recv_sem=out_recv.at[h, 0],
                device_id=(f, yy * 2 + xhi), device_id_type=MESH,
            ).start()

        for row, sem, xx in ((0, 1, xm), (1, 2, xp)):
            pltpu.make_async_remote_copy(
                src_ref=stage.at[h, yy, 1 - xhi, row], dst_ref=A.at[row + 2, :, mine],
                send_sem=out_send.at[h, sem], recv_sem=out_recv.at[h, sem],
                device_id=((xx % 2) * 16 + z * 2 + c, yy * 2 + xx // 2), device_id_type=MESH,
            ).start()

    def attend(h):
        def block(b, carry):
            yy = (y + 1 + b) % 4
            qq = inb[h, pl.ds(2 * yy, 2), :, 0:256].reshape(256, 256)
            kk = inb[h, :, :, 256:512].reshape(1024, 256)
            vv = inb[h, :, :, 512:768].reshape(1024, 256)
            nt = (((1,), (1,)), ((), ()))
            scores = lax.dot_general(qq[:, 128:], kk[:, :128], nt, preferred_element_type=F32)
            scores_dot = lax.dot_general(qq, kk, nt, preferred_element_type=F32)
            peak = jnp.max(scores, axis=1, keepdims=True)
            expo = jnp.exp((scores - peak) * SCALE)
            inv = 1.0 / jnp.sum(expo, axis=1, keepdims=True)
            mean = jnp.sum(expo * scores_dot, axis=1, keepdims=True) * inv
            probs = expo * inv
            probs_dot = (expo * (inv * SCALE)) * (scores_dot - mean)
            both = jnp.dot(probs.astype(BF16), vv, preferred_element_type=F32)
            out_dot = both[:, 128:] + jnp.dot(probs_dot.astype(BF16), vv[:, :128], preferred_element_type=F32)
            stage[h, yy, :, 0] = both[:, :128].astype(BF16).reshape(2, 128, HD)
            stage[h, yy, :, 1] = out_dot.astype(BF16).reshape(2, 128, HD)
            send_out(h, yy)
            return carry

        lax.fori_loop(0, 4, block, 0)

    def wait_bytes(part, sem):
        pltpu.make_async_copy(part, part, sem).wait()

    def forward(h, i, src_row, dst_row, hi, dx):
        pltpu.make_async_remote_copy(
            src_ref=A.at[src_row, :, lanes_of(h, hi)], dst_ref=A.at[dst_row, :, lanes_of(h, hi)],
            send_sem=fsend.at[h, i], recv_sem=frecv.at[h, i],
            device_id=dev(dx=dx), device_id_type=MESH,
        ).start()

    def relay_out(h):
        wait_bytes(stage.at[h, pl.ds(0, 3), 0], out_recv.at[h, 0])
        forward(h, 0, 0, 2, xhi, 1)
        forward(h, 1, 1, 3, xhi, 3)
        wait_bytes(A.at[2, :, lanes_of(h, xp // 2)], out_recv.at[h, 1])
        forward(h, 2, 2, 0, xp // 2, 3)
        wait_bytes(A.at[3, :, lanes_of(h, xm // 2)], out_recv.at[h, 2])
        forward(h, 3, 3, 1, xm // 2, 1)

    def wait_out(h):
        wait_bytes(A.at[2, :, lanes_of(h, xm // 2)], frecv.at[h, 0])
        wait_bytes(A.at[3, :, lanes_of(h, xp // 2)], frecv.at[h, 1])
        wait_bytes(A.at[0, :, lanes_of(h, 1 - xhi)], frecv.at[h, 2])
        wait_bytes(A.at[1, :, lanes_of(h, 1 - xhi)], frecv.at[h, 3])

    def prepare_send():
        pltpu.make_async_copy(w, wo, osem.at[5]).start()
        pltpu.make_async_remote_copy(
            src_ref=w, dst_ref=wx, send_sem=osem.at[1], recv_sem=osem.at[2],
            device_id=mate, device_id_type=MESH,
        ).start()

    def prepare():
        row = lax.broadcasted_iota(jnp.int32, (192, 384), 0)
        lane = lax.broadcasted_iota(jnp.int32, (192, 384), 1)
        put_own = (lane == row + 192 * c).astype(BF16)
        put_other = (lane == row + 192 * peer).astype(BF16)
        tn = (((0,), (0,)), ((), ()))
        wait_bytes(wo, osem.at[5])
        both = lax.dot_general(wo[...], put_own, tn, preferred_element_type=F32)
        wait_bytes(wx, osem.at[2])
        both += lax.dot_general(wx[...], put_other, tn, preferred_element_type=F32)
        wide[...] = both.astype(BF16).reshape(3, 2, 64, 384)
        W[z, :, xhi, y, c] = wide[:, c]

    def chunk(slab, turn, core=None):
        return W.at[slab, :, :, (y + turn) % 4, c if core is None else core]

    plane = {}
    ring = {}
    mates = {}

    def plane_x():
        plane["x"] = push(W.at[z, :, xhi, y, c], dev(dx=2))

    def plane_y():
        landed(W.at[z, :, 1 - xhi, y, c], plane["x"])
        for turn in (1, 3, 2):
            plane[turn] = push(chunk(z, 0), dev(dy=4 - turn))

    def ring_start(j):
        turn = TURNS[j]
        if turn:
            landed(chunk(z, turn), plane[turn])
        ring[0, 0, j] = push(chunk(z, turn), dev(dz=1))
        ring[1, 0, j] = push(chunk(z, turn), dev(dz=7))
        mates["own", j] = push(chunk(z, turn), mate)

    def slab_of(way, step):
        return (z + 7 - step) % 8 if way == 0 else (z + 1 + step) % 8

    def ways(step, j):
        return (0, 1) if step < 3 else ((0,) if j < 2 else (1,))

    def ring_turn(step, j):
        for way in ways(step, j):
            part = chunk(slab_of(way, step), TURNS[j])
            landed(part, ring[way, step, j])
            if step < 3 and way in ways(step + 1, j):
                ring[way, step + 1, j] = push(part, dev(dz=1 if way == 0 else 7))
            mates[way, step, j] = push(part, mate)

    def slab_wait(way, step):
        for j in range(4):
            if step is None:
                landed(chunk(z, TURNS[j], peer), mates["own", j])
            elif step < 3:
                landed(chunk(slab_of(way, step), TURNS[j], peer), mates[way, step, j])
            else:
                own_way = ways(3, j)[0]
                landed(chunk(slab_of(own_way, 3), TURNS[j], peer), mates[own_way, 3, j])

    def project(n):
        total = jnp.dot(A[...].reshape(512, 3072), W[n].reshape(3072, 384), preferred_element_type=F32)
        ob[n] = total.astype(BF16).reshape(4, 128, 384)
        columns = pl.ds(pl.multiple_of(xlo * 3072 + n * 384, HD), 384)
        for row, ref, dx in ((2, mixed, 3), (3, mixed_dot, 1)):
            pltpu.make_async_remote_copy(
                src_ref=ob.at[n, row], dst_ref=ref.at[0, :, columns],
                send_sem=osem.at[3], recv_sem=osem.at[4],
                device_id=dev(dx=dx), device_id_type=MESH,
            ).start()
        for row, ref in ((0, mixed), (1, mixed_dot)):
            pltpu.make_async_copy(ob.at[n, row], ref.at[0, :, columns], osem.at[0]).start()

    def project_pair(step):
        def one(way, carry):
            project((z + 7 - step + way * (2 + 2 * step)) % 8)
            return carry

        lax.fori_loop(0, 2, one, 0)

    prepare_send()
    prepare()
    plane_x()
    send_in_x(0)
    send_in_x(1)
    plane_y()
    ring_start(0)
    send_in(0)
    send_in(1)
    send_in_x(2)
    send_in(2)
    ring_start(1)
    ring_start(2)
    ring_start(3)
    ring_turn(0, 0)
    ring_turn(0, 1)
    wait_in(0)
    attend(0)
    ring_turn(0, 2)
    ring_turn(0, 3)
    ring_turn(1, 0)
    ring_turn(1, 1)
    wait_in(1)
    attend(1)
    relay_out(0)
    ring_turn(1, 2)
    ring_turn(1, 3)
    wait_in(2)
    attend(2)
    relay_out(1)
    ring_turn(2, 0)
    ring_turn(2, 1)
    relay_out(2)
    slab_wait(0, None)
    for h in range(3):
        wait_out(h)
    project(z)
    ring_turn(2, 2)
    slab_wait(0, 0)
    slab_wait(1, 0)
    project_pair(0)
    ring_turn(2, 3)
    slab_wait(0, 1)
    slab_wait(1, 1)
    project_pair(1)
    slab_wait(0, 2)
    slab_wait(1, 2)
    project_pair(2)
    for j in range(4):
        ring_turn(3, j)
    slab_wait(0, 3)
    project((z + 4) % 8)

    wait_bytes(ob.at[:, pl.ds(0, 2)], osem.at[4])
    wait_bytes(ob.at[:, pl.ds(0, 2)], osem.at[3])
    wait_bytes(ob.at[:, pl.ds(0, 2)], osem.at[0])
    wait_bytes(wx, osem.at[1])
    for h in range(3):
        wait_bytes(inb.at[h, pl.ds(0, 7)], in_send.at[h])
        wait_bytes(stage.at[h, pl.ds(0, 3), 0], out_send.at[h, 0])
        for i in (1, 2):
            wait_bytes(A.at[2, :, lanes_of(h, 0)], out_send.at[h, i])
        for i in range(4):
            wait_bytes(A.at[0, :, lanes_of(h, 0)], fsend.at[h, i])
    for part, sem in sent:
        wait_bytes(part, wsend.at[sem])
    assert count[0] <= wsend.shape[0] and len(sent) == count[0]


def body(queries, keys, values, query_tangent, key_tangent, value_tangent, out_weight):
    any_space = pl.BlockSpec(memory_space=pl.ANY)
    shape = jax.ShapeDtypeStruct((1, 128, 6144), BF16)
    return pl.pallas_call(
        kernel,
        name="attend_project",
        out_shape=(shape, shape),
        in_specs=[any_space] * 7,
        out_specs=(any_space, any_space),
        scratch_shapes=[
            pltpu.VMEM((8, 3, 2, 4, 2, 64, 384), BF16),
            pltpu.VMEM((3, 8, 128, 768), BF16),
            pltpu.VMEM((3, 4, 2, 2, 128, 128), BF16),
            pltpu.VMEM((4, 128, 3072), BF16),
            pltpu.VMEM((8, 4, 128, 384), BF16),
            pltpu.VMEM((192, 384), BF16),
            pltpu.VMEM((192, 384), BF16),
            pltpu.VMEM((3, 2, 64, 384), BF16),
            pltpu.SemaphoreType.DMA((3,)),
            pltpu.SemaphoreType.DMA((3,)),
            pltpu.SemaphoreType.DMA((3,)),
            pltpu.SemaphoreType.DMA((3, 3)),
            pltpu.SemaphoreType.DMA((3, 3)),
            pltpu.SemaphoreType.DMA((3, 4)),
            pltpu.SemaphoreType.DMA((3, 4)),
            pltpu.SemaphoreType.DMA((96,)),
            pltpu.SemaphoreType.DMA((96,)),
            pltpu.SemaphoreType.DMA((6,)),
        ],
        compiler_params=pltpu.CompilerParams(
            collective_id=0, has_side_effects=True, vmem_limit_bytes=56 * 2**20
        ),
        cost_estimate=pl.CostEstimate(
            flops=17 * 10**9, bytes_accessed=8 * 2**20, transcendentals=3 * 2**20
        ),
    )(queries, keys, values, query_tangent, key_tangent, value_tangent, out_weight.T)


def solution(mesh):
    placed = (P("fsdp", "seq", None),) * 6 + (P("seq", "fsdp"),)
    return jax.shard_map(
        body,
        mesh=mesh,
        in_specs=placed,
        out_specs=(P("fsdp", "seq", None), P("fsdp", "seq", None)),
        check_vma=False,
    )
```

```python
import math

import jax
import jax.numpy as jnp
from jax import lax
from jax.experimental import pallas as pl
from jax.experimental.pallas import tpu as pltpu
from jax.sharding import PartitionSpec as P

HD = 128
MESH = pl.DeviceIdType.MESH
F32 = jnp.float32
BF16 = jnp.bfloat16
SCALE = 1.0 / math.sqrt(HD)
TURNS = (0, 1, 3, 2)


def kernel(q, k, v, qd, kd, vd, w, mixed, mixed_dot, W, inb, stage, A, ob, wx, wo, wide,
           in_send, in_recv, in_loc, out_send, out_recv, fsend, frecv, wsend, wrecv, osem):
    f, s = lax.axis_index("fsdp"), lax.axis_index("seq")
    xlo, z, c = f // 16, (f // 2) % 8, f % 2
    y, xhi = s // 2, s % 2
    x = xhi * 2 + xlo
    peer = 1 - c
    xm, xp = (x + 3) % 4, (x + 1) % 4

    def dev(dx=0, dy=0, dz=0, core=None):
        xx, yy, zz = (x + dx) % 4, (y + dy) % 4, (z + dz) % 8
        return ((xx % 2) * 16 + zz * 2 + (c if core is None else core), yy * 2 + xx // 2)

    mate = dev(core=peer)

    barrier = pltpu.get_barrier_semaphore()

    def greet(device):
        pl.semaphore_signal(barrier, inc=1, device_id=device, device_id_type=MESH)

    def greet_seq(j, carry):
        greet((f, (s + j) % 8))
        return carry

    def greet_x(j, carry):
        greet(dev(dx=1, dy=j))
        greet(dev(dx=3, dy=j))
        return carry

    lax.fori_loop(1, 8, greet_seq, 0)
    lax.fori_loop(0, 4, greet_x, 0)
    greet(dev(dz=1))
    greet(dev(dz=7))
    greet(mate)
    pl.semaphore_wait(barrier, 18)

    count = [0]
    sent = []

    def push(part, device):
        sem = count[0]
        count[0] += 1
        pltpu.make_async_remote_copy(
            src_ref=part, dst_ref=part, send_sem=wsend.at[sem], recv_sem=wrecv.at[sem],
            device_id=device, device_id_type=MESH,
        ).start()
        return sem

    def landed(part, sem):
        pltpu.make_async_copy(part, part, wrecv.at[sem]).wait()
        sent.append((part, sem))

    arrays = (qd, q, k, kd, v, vd)

    def send_in_to(h, t):
        for i, ref in enumerate(arrays):
            pltpu.make_async_remote_copy(
                src_ref=ref.at[0, :, pl.ds(pl.multiple_of(t * 384 + h * HD, HD), HD)],
                dst_ref=inb.at[h, s, :, pl.ds(i * HD, HD)],
                send_sem=in_send.at[h], recv_sem=in_recv.at[h],
                device_id=(f, t), device_id_type=MESH,
            ).start()

    def send_in_x(h):
        send_in_to(h, 2 * y + 1 - xhi)

    def send_in(h):
        def to(j, carry):
            send_in_to(h, (2 * y + j) % 8)
            return carry

        lax.fori_loop(2, 8, to, 0)
        for i, ref in enumerate(arrays):
            pltpu.make_async_copy(
                ref.at[0, :, pl.ds(pl.multiple_of(s * 384 + h * HD, HD), HD)],
                inb.at[h, s, :, pl.ds(i * HD, HD)],
                in_loc.at[h],
            ).start()

    def wait_in(h):
        pltpu.make_async_copy(inb.at[h, pl.ds(0, 7)], inb.at[h, pl.ds(0, 7)], in_recv.at[h]).wait()
        pltpu.make_async_copy(inb.at[h, s], inb.at[h, s], in_loc.at[h]).wait()

    def lane_of(h, hi, yy):
        return pl.ds(pl.multiple_of(((h * 2 + hi) * 4 + yy) * HD, HD), HD)

    def lanes_of(h, hi):
        return pl.ds(pl.multiple_of((h * 2 + hi) * 512, 512), 512)

    def send_out(h, yy):
        mine = lane_of(h, xhi, y)

        @pl.when(yy == y)
        def _():
            A[0:2, :, mine] = stage[h, yy, xhi]

        @pl.when(yy != y)
        def _():
            pltpu.make_async_remote_copy(
                src_ref=stage.at[h, yy, xhi], dst_ref=A.at[pl.ds(0, 2), :, mine],
                send_sem=out_send.at[h, 0], recv_sem=out_recv.at[h, 0],
                device_id=(f, yy * 2 + xhi), device_id_type=MESH,
            ).start()

        for row, sem, xx in ((0, 1, xm), (1, 2, xp)):
            pltpu.make_async_remote_copy(
                src_ref=stage.at[h, yy, 1 - xhi, row], dst_ref=A.at[row + 2, :, mine],
                send_sem=out_send.at[h, sem], recv_sem=out_recv.at[h, sem],
                device_id=((xx % 2) * 16 + z * 2 + c, yy * 2 + xx // 2), device_id_type=MESH,
            ).start()

    def attend(h):
        def block(b, carry):
            yy = (y + 1 + b) % 4
            qq = inb[h, pl.ds(2 * yy, 2), :, 0:256].reshape(256, 256)
            kk = inb[h, :, :, 256:512].reshape(1024, 256)
            vv = inb[h, :, :, 512:768].reshape(1024, 256)
            nt = (((1,), (1,)), ((), ()))
            scores = lax.dot_general(qq[:, 128:], kk[:, :128], nt, preferred_element_type=F32)
            scores_dot = lax.dot_general(qq, kk, nt, preferred_element_type=F32)
            peak = jnp.max(scores, axis=1, keepdims=True)
            expo = jnp.exp((scores - peak) * SCALE)
            inv = 1.0 / jnp.sum(expo, axis=1, keepdims=True)
            mean = jnp.sum(expo * scores_dot, axis=1, keepdims=True) * inv
            probs = expo * inv
            probs_dot = (expo * (inv * SCALE)) * (scores_dot - mean)
            both = jnp.dot(probs.astype(BF16), vv, preferred_element_type=F32)
            out_dot = both[:, 128:] + jnp.dot(probs_dot.astype(BF16), vv[:, :128], preferred_element_type=F32)
            stage[h, yy, :, 0] = both[:, :128].astype(BF16).reshape(2, 128, HD)
            stage[h, yy, :, 1] = out_dot.astype(BF16).reshape(2, 128, HD)
            send_out(h, yy)
            return carry

        lax.fori_loop(0, 4, block, 0)

    def wait_bytes(part, sem):
        pltpu.make_async_copy(part, part, sem).wait()

    def forward(h, i, src_row, dst_row, hi, dx):
        pltpu.make_async_remote_copy(
            src_ref=A.at[src_row, :, lanes_of(h, hi)], dst_ref=A.at[dst_row, :, lanes_of(h, hi)],
            send_sem=fsend.at[h, i], recv_sem=frecv.at[h, i],
            device_id=dev(dx=dx), device_id_type=MESH,
        ).start()

    def relay_out(h):
        wait_bytes(stage.at[h, pl.ds(0, 3), 0], out_recv.at[h, 0])
        forward(h, 0, 0, 2, xhi, 1)
        forward(h, 1, 1, 3, xhi, 3)
        wait_bytes(A.at[2, :, lanes_of(h, xp // 2)], out_recv.at[h, 1])
        forward(h, 2, 2, 0, xp // 2, 3)
        wait_bytes(A.at[3, :, lanes_of(h, xm // 2)], out_recv.at[h, 2])
        forward(h, 3, 3, 1, xm // 2, 1)

    def wait_out(h):
        wait_bytes(A.at[2, :, lanes_of(h, xm // 2)], frecv.at[h, 0])
        wait_bytes(A.at[3, :, lanes_of(h, xp // 2)], frecv.at[h, 1])
        wait_bytes(A.at[0, :, lanes_of(h, 1 - xhi)], frecv.at[h, 2])
        wait_bytes(A.at[1, :, lanes_of(h, 1 - xhi)], frecv.at[h, 3])

    def prepare_send():
        pltpu.make_async_copy(w, wo, osem.at[5]).start()
        pltpu.make_async_remote_copy(
            src_ref=w, dst_ref=wx, send_sem=osem.at[1], recv_sem=osem.at[2],
            device_id=mate, device_id_type=MESH,
        ).start()

    def prepare():
        row = lax.broadcasted_iota(jnp.int32, (192, 384), 0)
        lane = lax.broadcasted_iota(jnp.int32, (192, 384), 1)
        put_own = (lane == row + 192 * c).astype(BF16)
        put_other = (lane == row + 192 * peer).astype(BF16)
        tn = (((0,), (0,)), ((), ()))
        wait_bytes(wo, osem.at[5])
        both = lax.dot_general(wo[...], put_own, tn, preferred_element_type=F32)
        wait_bytes(wx, osem.at[2])
        both += lax.dot_general(wx[...], put_other, tn, preferred_element_type=F32)
        wide[...] = both.astype(BF16).reshape(3, 2, 64, 384)
        W[z, :, xhi, y, c] = wide[:, c]

    def chunk(slab, turn, core=None):
        return W.at[slab, :, :, (y + turn) % 4, c if core is None else core]

    plane = {}
    ring = {}
    mates = {}

    def plane_x():
        plane["x"] = push(W.at[z, :, xhi, y, c], dev(dx=2))

    def plane_y():
        landed(W.at[z, :, 1 - xhi, y, c], plane["x"])
        for turn in (1, 3):
            plane[turn] = push(chunk(z, 0), dev(dy=4 - turn))

    def plane_y_far():
        plane[2] = push(chunk(z, 0), dev(dy=2))

    def ring_start(j):
        turn = TURNS[j]
        if turn:
            landed(chunk(z, turn), plane[turn])
        ring[0, 0, j] = push(chunk(z, turn), dev(dz=1))
        ring[1, 0, j] = push(chunk(z, turn), dev(dz=7))
        mates["own", j] = push(chunk(z, turn), mate)

    def slab_of(way, step):
        return (z + 7 - step) % 8 if way == 0 else (z + 1 + step) % 8

    def ways(step, j):
        return (0, 1) if step < 3 else ((0,) if j < 2 else (1,))

    def ring_turn(step, j):
        for way in ways(step, j):
            part = chunk(slab_of(way, step), TURNS[j])
            landed(part, ring[way, step, j])
            if step < 3 and way in ways(step + 1, j):
                ring[way, step + 1, j] = push(part, dev(dz=1 if way == 0 else 7))
            mates[way, step, j] = push(part, mate)

    def slab_wait(way, step):
        for j in range(4):
            if step is None:
                landed(chunk(z, TURNS[j], peer), mates["own", j])
            elif step < 3:
                landed(chunk(slab_of(way, step), TURNS[j], peer), mates[way, step, j])
            else:
                own_way = ways(3, j)[0]
                landed(chunk(slab_of(own_way, 3), TURNS[j], peer), mates[own_way, 3, j])

    def project(n):
        total = jnp.dot(A[...].reshape(512, 3072), W[n].reshape(3072, 384), preferred_element_type=F32)
        ob[n] = total.astype(BF16).reshape(4, 128, 384)
        columns = pl.ds(pl.multiple_of(xlo * 3072 + n * 384, HD), 384)
        for row, ref, dx in ((2, mixed, 3), (3, mixed_dot, 1)):
            pltpu.make_async_remote_copy(
                src_ref=ob.at[n, row], dst_ref=ref.at[0, :, columns],
                send_sem=osem.at[3], recv_sem=osem.at[4],
                device_id=dev(dx=dx), device_id_type=MESH,
            ).start()
        for row, ref in ((0, mixed), (1, mixed_dot)):
            pltpu.make_async_copy(ob.at[n, row], ref.at[0, :, columns], osem.at[0]).start()

    def project_pair(step):
        def one(way, carry):
            project((z + 7 - step + way * (2 + 2 * step)) % 8)
            return carry

        lax.fori_loop(0, 2, one, 0)

    prepare_send()
    prepare()
    plane_x()
    send_in_x(0)
    send_in_x(1)
    plane_y()
    ring_start(0)
    send_in(0)
    plane_y_far()
    send_in(1)
    send_in_x(2)
    send_in(2)
    ring_start(1)
    ring_start(2)
    ring_start(3)
    ring_turn(0, 0)
    ring_turn(0, 1)
    wait_in(0)
    attend(0)
    ring_turn(0, 2)
    ring_turn(0, 3)
    ring_turn(1, 0)
    ring_turn(1, 1)
    wait_in(1)
    attend(1)
    relay_out(0)
    ring_turn(1, 2)
    ring_turn(1, 3)
    wait_in(2)
    attend(2)
    relay_out(1)
    ring_turn(2, 0)
    ring_turn(2, 1)
    relay_out(2)
    slab_wait(0, None)
    for h in range(3):
        wait_out(h)
    project(z)
    ring_turn(2, 2)
    slab_wait(0, 0)
    slab_wait(1, 0)
    project_pair(0)
    ring_turn(2, 3)
    slab_wait(0, 1)
    slab_wait(1, 1)
    project_pair(1)
    slab_wait(0, 2)
    slab_wait(1, 2)
    project_pair(2)
    for j in range(4):
        ring_turn(3, j)
    slab_wait(0, 3)
    project((z + 4) % 8)

    wait_bytes(ob.at[:, pl.ds(0, 2)], osem.at[4])
    wait_bytes(ob.at[:, pl.ds(0, 2)], osem.at[3])
    wait_bytes(ob.at[:, pl.ds(0, 2)], osem.at[0])
    wait_bytes(wx, osem.at[1])
    for h in range(3):
        wait_bytes(inb.at[h, pl.ds(0, 7)], in_send.at[h])
        wait_bytes(stage.at[h, pl.ds(0, 3), 0], out_send.at[h, 0])
        for i in (1, 2):
            wait_bytes(A.at[2, :, lanes_of(h, 0)], out_send.at[h, i])
        for i in range(4):
            wait_bytes(A.at[0, :, lanes_of(h, 0)], fsend.at[h, i])
    for part, sem in sent:
        wait_bytes(part, wsend.at[sem])
    assert count[0] <= wsend.shape[0] and len(sent) == count[0]


def body(queries, keys, values, query_tangent, key_tangent, value_tangent, out_weight):
    any_space = pl.BlockSpec(memory_space=pl.ANY)
    shape = jax.ShapeDtypeStruct((1, 128, 6144), BF16)
    return pl.pallas_call(
        kernel,
        name="attend_project",
        out_shape=(shape, shape),
        in_specs=[any_space] * 7,
        out_specs=(any_space, any_space),
        scratch_shapes=[
            pltpu.VMEM((8, 3, 2, 4, 2, 64, 384), BF16),
            pltpu.VMEM((3, 8, 128, 768), BF16),
            pltpu.VMEM((3, 4, 2, 2, 128, 128), BF16),
            pltpu.VMEM((4, 128, 3072), BF16),
            pltpu.VMEM((8, 4, 128, 384), BF16),
            pltpu.VMEM((192, 384), BF16),
            pltpu.VMEM((192, 384), BF16),
            pltpu.VMEM((3, 2, 64, 384), BF16),
            pltpu.SemaphoreType.DMA((3,)),
            pltpu.SemaphoreType.DMA((3,)),
            pltpu.SemaphoreType.DMA((3,)),
            pltpu.SemaphoreType.DMA((3, 3)),
            pltpu.SemaphoreType.DMA((3, 3)),
            pltpu.SemaphoreType.DMA((3, 4)),
            pltpu.SemaphoreType.DMA((3, 4)),
            pltpu.SemaphoreType.DMA((96,)),
            pltpu.SemaphoreType.DMA((96,)),
            pltpu.SemaphoreType.DMA((6,)),
        ],
        compiler_params=pltpu.CompilerParams(
            collective_id=0, has_side_effects=True, vmem_limit_bytes=56 * 2**20
        ),
        cost_estimate=pl.CostEstimate(
            flops=17 * 10**9, bytes_accessed=8 * 2**20, transcendentals=3 * 2**20
        ),
    )(queries, keys, values, query_tangent, key_tangent, value_tangent, out_weight.T)


def solution(mesh):
    placed = (P("fsdp", "seq", None),) * 6 + (P("seq", "fsdp"),)
    return jax.shard_map(
        body,
        mesh=mesh,
        in_specs=placed,
        out_specs=(P("fsdp", "seq", None), P("fsdp", "seq", None)),
        check_vma=False,
    )
```
